512 devices in a mesh: dom: 16 (over z), row: 8 (over y, core), col: 4 (over x).
Axes of the slice: x: 4, y: 4, z: 16, core: 2. Of those that a mesh axis runs over, the one named last changes fastest.
Arguments:
- protein_panel: float32 [8, 4, 128, 16384], P('row', 'col', None, 'dom'), may hold values from 0 to 0.03125
- tile_mask: int32 [8, 4, 1, 128], P('row', 'col', None, 'dom'), may hold values 0 or 1
- domain_class: int32 [16384], P('dom'), may hold values from 0 to 15
- class_weight: float32 [16], replicated, may hold values from 0.1 to 1
Outputs:
- flow: float32 [8, 4, 128, 8, 4, 128], P('row', None, 'dom', None, 'col')
The draws below stay inside these ranges and needn't reach their ends.
All inputs are finite; a program needn't handle non-finite values. No bound on the sum of `tile_mask` on one device may be relied on, other than what follows from the above.
Results may differ from the reference program's by a relative error of at most 0.00005.
Values sent between devices are 32-bit elements; how exact they have to be, the bound alone decides.
No kernel may reach another device: no remote copies, remote signals or barrier semaphores. Data moves between devices by JAX's collectives and lax.ppermute only.
A program may use at most 64 MiB of HBM per device.

```python
import math
import jax
import jax.numpy as jnp
from jax import lax

TILE = 128
PL = 128
CLASSES = 16
PROT = 4096
DOMS = 16384
N_ROW = 8
N_COL = 4


def touch_ends(drawn, key, least, largest):
    place = [jax.random.randint(jax.random.fold_in(key, axis), (), 0, length) for axis, length in enumerate(drawn.shape)]
    main_axis = drawn.shape.index(max(drawn.shape))
    neighbour = place[:main_axis] + [(place[main_axis] + 1) % drawn.shape[main_axis]] + place[main_axis + 1:]
    return drawn.at[tuple(place)].set(least).at[tuple(neighbour)].set(largest)


def steps_of(key, dims, pieces, least, top_value):
    loudness = 1.0
    for axis_at, parts in pieces:
        heights = jax.random.uniform(jax.random.fold_in(jax.random.fold_in(key, 6), axis_at), (parts,), jnp.float32, least / len(pieces), top_value / len(pieces))
        loudness = loudness * jnp.repeat(jnp.exp(heights), dims[axis_at] // parts).reshape((-1,) + (1,) * (len(dims) - 1 - axis_at))
    return loudness


def setup_inputs(seed: int = 0) -> dict:
    seeds = jax.random.split(jax.random.key(seed), 5)
    return {
        "protein_panel": jnp.clip(0.03125 * jax.random.uniform(seeds[0], (N_ROW, N_COL, PL, DOMS), jnp.float32) ** steps_of(seeds[0], (N_ROW, N_COL, PL, DOMS), ((0, 8), (1, 4), (3, 16)), -0.2, 0.2), 0.0, 0.03125),
        "tile_mask": touch_ends((jax.random.randint(seeds[1], (N_ROW, N_COL, PL // TILE, DOMS // TILE), 0, 4) < 1).astype(jnp.int32), jax.random.fold_in(seeds[1], 1), 0, 1),
        "domain_class": touch_ends(jax.random.randint(seeds[2], (DOMS,), 0, CLASSES), jax.random.fold_in(seeds[2], 1), 0, CLASSES - 1).astype(jnp.int32),
        "class_weight": jnp.clip(jnp.exp(jax.random.uniform(seeds[3], (CLASSES,), jnp.float32, math.log(0.1), math.log(1.0))), 0.1, 1.0),
    }


def reference(protein_panel, tile_mask, domain_class, class_weight):
    expanded = jnp.repeat(jnp.repeat(tile_mask.astype(jnp.float32), TILE, axis=2), TILE, axis=3)
    scores = (protein_panel * expanded).reshape(PROT, DOMS)
    weights = class_weight[domain_class]
    similar = jnp.dot(scores * weights[None, :], scores.T, precision=lax.Precision.HIGHEST, preferred_element_type=jnp.float32)
    similar = similar + jnp.eye(PROT, dtype=jnp.float32)
    totals = jnp.sum(similar, axis=0)
    flow = similar * (PROT / totals)[None, :]
    return flow.reshape(N_ROW, N_COL, PL, N_ROW, N_COL, PL)
```

```python
import jax
import jax.numpy as jnp
from jax import lax
from jax.sharding import PartitionSpec as P

TILE = 128


def per_device(protein_panel, tile_mask, domain_class, class_weight):
    n_rows = lax.axis_size("row")
    n_cols = lax.axis_size("col")
    n_doms = lax.axis_size("dom")
    width = protein_panel.shape[2]
    panel_cols = protein_panel.shape[3]
    local_rows = width // n_doms
    tiles_cols = panel_cols // TILE
    mask = jnp.broadcast_to(
        tile_mask.astype(jnp.float32).reshape(tiles_cols, 1), (tiles_cols, TILE)
    ).reshape(1, panel_cols)
    masked = protein_panel.reshape(width, panel_cols) * mask
    one_hot = (
        domain_class[:, None] == jnp.arange(class_weight.shape[0], dtype=jnp.int32)[None, :]
    ).astype(jnp.float32)
    weights = jnp.dot(one_hot, class_weight, precision=lax.Precision.HIGHEST)
    q = lax.all_gather(masked, "row", axis=0, tiled=True)
    sums = lax.psum(jnp.sum(q, axis=0), "col")
    p = lax.all_gather(masked, "col", axis=0)
    shares = jnp.einsum(
        "d,qd->q", sums * weights, q, precision=lax.Precision.HIGHEST
    )
    weighted = p.reshape(n_cols, n_doms, local_rows, panel_cols) * weights
    weighted = jnp.transpose(weighted, (1, 0, 2, 3)).reshape(n_cols * width, panel_cols)
    block = jnp.einsum("pd,qd->pq", weighted, q, precision=lax.Precision.HIGH)
    block = block.reshape(n_doms, n_cols * local_rows, n_rows * width)
    extra = jnp.broadcast_to(shares[None, None, :], (n_doms, 8, n_rows * width))
    block = lax.psum_scatter(
        jnp.concatenate([block, extra], axis=1), "dom", scatter_dimension=0, tiled=False
    )
    totals = block[n_cols * local_rows] + 1.0
    block = block[: n_cols * local_rows].reshape(n_cols, local_rows, n_rows, width)
    grid_shape = (n_cols, local_rows, n_rows, width)
    diagonal = (
        (lax.broadcasted_iota(jnp.int32, grid_shape, 0) == lax.axis_index("col"))
        & (lax.broadcasted_iota(jnp.int32, grid_shape, 2) == lax.axis_index("row"))
        & (
            lax.broadcasted_iota(jnp.int32, grid_shape, 3)
            == lax.axis_index("dom") * local_rows
            + lax.broadcasted_iota(jnp.int32, grid_shape, 1)
        )
    )
    scaling = n_rows * n_cols * width / totals.reshape(n_rows, width)
    flow = (block + diagonal.astype(jnp.float32)) * scaling[None, None, :, :]
    return flow.reshape(1, n_cols, local_rows, n_rows, 1, width)


def solution(mesh):
    placed = (P("row", "col", None, "dom"), P("row", "col", None, "dom"), P("dom"), P())
    return jax.shard_map(
        per_device,
        mesh=mesh,
        in_specs=placed,
        out_specs=P("row", None, "dom", None, "col", None),
        check_vma=False,
    )
```

```python
import functools

import jax
import jax.numpy as jnp
from jax import lax
from jax.experimental import pallas as pl
from jax.experimental.pallas import tpu as pltpu
from jax.sharding import PartitionSpec as P

TILE = 128
N_DOM, N_ROW, N_COL = 16, 8, 4
WIDTH = 128
PANEL = 1024
POS = WIDTH // N_DOM
UNIT = N_COL * 2 * POS
HALF = 4 * WIDTH
PROT = N_ROW * N_COL * WIDTH
PARAMS = pltpu.CompilerParams(vmem_limit_bytes=32 * 1024 * 1024)
VMEM = pl.BlockSpec(memory_space=pltpu.VMEM)
SMEM = pl.BlockSpec(memory_space=pltpu.SMEM)
F32 = jnp.float32
BF16 = jnp.bfloat16


def call(body, outs, in_specs, flops=0, nbytes=0, scratch=()):
    many = isinstance(outs, list)
    return pl.pallas_call(
        body,
        out_shape=[jax.ShapeDtypeStruct(s, F32) for s in outs] if many else jax.ShapeDtypeStruct(outs, F32),
        in_specs=in_specs,
        out_specs=[VMEM] * len(outs) if many else VMEM,
        scratch_shapes=list(scratch),
        compiler_params=PARAMS,
        cost_estimate=pl.CostEstimate(flops=flops, bytes_accessed=nbytes, transcendentals=0),
    )


def mask_body(panel, tile_mask, classes, class_weight, own, weights):
    for t in range(PANEL // TILE):
        at = pl.ds(t * TILE, TILE)
        kept = panel[:, at] * tile_mask[0, t].astype(F32)
        own[pl.ds(0, WIDTH), at] = kept
        own[pl.ds(WIDTH, 8), at] = jnp.broadcast_to(jnp.sum(kept, axis=0, keepdims=True), (8, TILE))
    of = classes[...]
    found = jnp.zeros((1, PANEL), F32)
    for k in range(class_weight.shape[0]):
        found = jnp.where(of == k, class_weight[k], found)
    weights[...] = found


def pick_body(shards, own, other, weights, out):
    w = weights[...]
    for j in range(8):
        at = pl.ds(pl.multiple_of(shards[j] * POS, POS), POS)
        out[pl.ds(j * 2 * POS, POS), :] = own[at, :] * w
        out[pl.ds(j * 2 * POS + POS, POS), :] = other[at, :] * w


def split(x):
    high = x.astype(BF16)
    return high, (x - high.astype(F32)).astype(BF16)


def dot3(ph, pl_, qh, ql):
    dims = (((1,), (1,)), ((), ()))
    dot = functools.partial(lax.dot_general, dimension_numbers=dims, preferred_element_type=F32)
    return dot(ph, qh) + (dot(ph, ql) + dot(pl_, qh))


def block_body(*refs, with_totals):
    if with_totals:
        ps, qs, rest, sums, weights = refs[:4], refs[4:8], refs[8:12], refs[12:16], refs[16]
        first, second, third, ph, pl_, qh, ql = refs[17:]
    else:
        ps, qs = refs[:4], refs[4:8]
        first, second, third, ph, pl_, qh, ql = refs[8:]
    for n in range(4):
        at = pl.ds(n * WIDTH, WIDTH)
        ph[at, :], pl_[at, :] = split(ps[n][...])
        qh[at, :], ql[at, :] = split(qs[n][pl.ds(0, WIDTH), :])
    block = dot3(ph[...], pl_[...], qh[...], ql[...])
    for n in range(N_COL):
        for j in range(8):
            out = (first, second, third)[j % 3]
            rows = n * WIDTH + j * 2 * POS
            out[pl.ds((j // 3) * UNIT + n * 2 * POS, 2 * POS), :] = block[rows : rows + 2 * POS]
    if with_totals:
        total = (sums[0][...] + sums[1][...] + sums[2][...] + sums[3][...]) * weights[...]
        th, tl = split(jnp.concatenate([total, total], axis=0))
        of_second = dot3(th, tl, qh[...], ql[...])[:8]
        for n in range(4):
            at = pl.ds(n * WIDTH, WIDTH)
            qh[at, :], ql[at, :] = split(rest[n][pl.ds(0, WIDTH), :])
        of_first = dot3(th, tl, qh[...], ql[...])[:8]
        odd = lax.broadcasted_iota(jnp.int32, (8, HALF), 0) % 2 == 1
        share = jnp.where(odd, of_second, of_first)
        first[pl.ds(3 * UNIT, 8), :] = share
        second[pl.ds(3 * UNIT, 8), :] = share


def finish_body(place, f_a, f_b, g_a, g_b, out):
    x, y, core, z = place[0], place[1], place[2], place[3]
    total_a = f_b[pl.ds(UNIT, 1), :] + g_b[pl.ds(UNIT // 2 + 1, 1), :]
    total_b = f_b[pl.ds(UNIT + 1, 1), :] + g_b[pl.ds(UNIT // 2, 1), :]
    scale_a, scale_b = PROT / (total_a + 1.0), PROT / (total_b + 1.0)
    lanes = lax.broadcasted_iota(jnp.int32, (POS, WIDTH), 1)
    rows = lax.broadcasted_iota(jnp.int32, (POS, WIDTH), 0)
    unit = (lanes == z * POS + rows).astype(F32)
    for n in range(N_COL):
        c = (x + n) % N_COL
        mine, theirs = pl.ds(n * 2 * POS, POS), pl.ds(n * POS, POS)
        for m in range(4):
            at = pl.ds(m * WIDTH, WIDTH)
            row = 2 * ((y + m) % 4)
            a = f_a[mine, at] + g_b[theirs, at]
            if n == 0 and m == 0:
                a = a + unit
            b = f_b[mine, at] + g_a[theirs, at]
            base = c * (POS * N_ROW) + row
            out[pl.ds(base + core, POS, stride=N_ROW), :] = a * scale_a[:, m * WIDTH : (m + 1) * WIDTH]
            out[pl.ds(base + 1 - core, POS, stride=N_ROW), :] = b * scale_b[:, m * WIDTH : (m + 1) * WIDTH]


def along_x(a, shift):
    return lax.ppermute(a, "col", [(i, (i + shift) % N_COL) for i in range(N_COL)])


def along_y(a, shift):
    return lax.ppermute(a, "row", [(i, (i + 2 * shift) % N_ROW) for i in range(N_ROW)])


def across(a):
    return lax.ppermute(a, "row", [(i, i ^ 1) for i in range(N_ROW)])


def along_z(a, shift):
    pairs = []
    for z in range(N_DOM):
        for r in range(N_ROW):
            to = (z + (shift if r % 2 == 0 else -shift)) % N_DOM
            pairs.append((z * N_ROW + r, to * N_ROW + r))
    return lax.ppermute(a, ("dom", "row"), pairs)


def per_device(protein_panel, tile_mask, domain_class, class_weight):
    x, r, z = lax.axis_index("col"), lax.axis_index("row"), lax.axis_index("dom")
    y, core = r // 2, r % 2
    steps = jnp.arange(8, dtype=jnp.int32)
    shards = jnp.where(
        core == 0, z + 8 - steps, jnp.where(steps == 0, z, z + 8 + steps)
    ) % N_DOM
    place = jnp.stack([x, y, core, z]).astype(jnp.int32)
    own, weights = call(
        mask_body, [(WIDTH + 8, PANEL), (1, PANEL)], [VMEM, SMEM, VMEM, SMEM], nbytes=1 << 20
    )(
        protein_panel.reshape(WIDTH, PANEL),
        tile_mask.reshape(1, PANEL // TILE),
        domain_class.reshape(1, PANEL),
        class_weight,
    )
    other = across(own)
    y_next = along_y(own, -1)
    y_last = along_y(own, 1)
    y_far = along_y(own, 2)
    picked = call(pick_body, (WIDTH, PANEL), [SMEM, VMEM, VMEM, VMEM], nbytes=3 << 19)(
        shards, own, other, weights
    )
    x_next = along_x(picked, -1)
    x_last = along_x(picked, 1)
    x_far = along_x(picked, 2)
    ps = (picked, x_next, x_far, x_last)
    qa = (own, y_next, y_far, y_last)
    qb = (other, across(y_next), across(y_far), across(y_last))
    halves = lambda count: [pltpu.VMEM((4 * WIDTH, PANEL), BF16) for _ in range(4)]
    flops = 6 * (4 * WIDTH) * HALF * PANEL
    a0, a1, a2 = call(
        functools.partial(block_body, with_totals=False),
        [(3 * UNIT, HALF), (3 * UNIT, HALF), (2 * UNIT, HALF)],
        [VMEM] * 8,
        flops=flops, nbytes=5 << 20, scratch=halves(4),
    )(*ps, *qa)
    ar = along_z(a0, 1)
    sums = sum(q[WIDTH:] for q in qa + qb)
    chips = (sums, along_x(sums, 1), along_x(sums, -1), along_x(sums, 2))
    b0, b1, b2 = call(
        functools.partial(block_body, with_totals=True),
        [(3 * UNIT + 8, HALF), (3 * UNIT + 8, HALF), (2 * UNIT, HALF)],
        [VMEM] * 17,
        flops=flops, nbytes=7 << 20, scratch=halves(4),
    )(*ps, *qb, *qa, *chips, weights)
    br = along_z(b0, 1)

    even = core == 0

    def second_step(u1, r1):
        return u1 + jnp.concatenate([jnp.where(even, r1[:UNIT], 0.0), r1[UNIT:]])

    a_sent = second_step(a1, ar)
    ar = along_z(a_sent, 1)
    b_sent = second_step(b1, br)
    br = along_z(b_sent, 1)
    a_near = a2[UNIT:] + ar[UNIT : 2 * UNIT]
    a_sum = ar[2 * UNIT :] + jnp.where(even, 0.0, a0[:UNIT])
    ar = along_z(a2[:UNIT] + ar[:UNIT], 3)
    share = b1[3 * UNIT :]
    b_near = b2[UNIT:] + br[UNIT : 2 * UNIT]
    b_sum = br[2 * UNIT : 3 * UNIT] + jnp.where(even, 0.0, b0[:UNIT])
    b_total = br[3 * UNIT :] + jnp.where(even, 0.0, share)
    narrow = (lax.broadcasted_iota(jnp.int32, (8, HALF), 0) >= 2) & ~even
    window = jnp.where(narrow, b_sent[3 * UNIT :], share + br[3 * UNIT :])
    br = along_z(jnp.concatenate([b2[:UNIT] + br[:UNIT], window]), 3)
    ar = along_z(a_near + ar, 3)
    b_total = b_total + br[UNIT:]
    br = along_z(jnp.concatenate([b_near + br[:UNIT], br[UNIT:]]), 3)
    f_a = a_sum + ar
    others = lambda f: f.reshape(N_COL, 2, POS, HALF)[:, 1].reshape(UNIT // 2, HALF)
    g_a = across(others(f_a))
    far = jnp.roll(br[UNIT:], -2, axis=0)
    f_b = jnp.concatenate([b_sum + br[:UNIT], b_total + far])
    g_b = across(jnp.concatenate([others(f_b[:UNIT]), f_b[UNIT:]]))
    flow = call(finish_body, (N_COL * POS * N_ROW, WIDTH), [SMEM] + [VMEM] * 4, nbytes=1 << 19)(
        place, f_a, f_b, g_a, g_b
    )
    return flow.reshape(1, N_COL, POS, N_ROW, 1, WIDTH)


def solution(mesh):
    placed = (P("row", "col", None, "dom"), P("row", "col", None, "dom"), P("dom"), P())
    return jax.shard_map(
        per_device,
        mesh=mesh,
        in_specs=placed,
        out_specs=P("row", None, "dom", None, "col", None),
        check_vma=False,
    )
```

```python
import functools

import jax
import jax.numpy as jnp
from jax import lax
from jax.experimental import pallas as pl
from jax.experimental.pallas import tpu as pltpu
from jax.sharding import PartitionSpec as P

TILE = 128
N_DOM, N_ROW, N_COL = 16, 8, 4
WIDTH = 128
PANEL = 1024
POS = WIDTH // N_DOM
PAIR = 2 * WIDTH
EARLY_ROWS, EARLY_COLS = 3 * 2 * POS, 3 * PAIR
LATE_ROWS, LATE_COLS = 2 * 2 * POS + 3 * POS, 2 * PAIR
TOTALS = 8
PART = N_COL * POS
PROT = N_ROW * N_COL * WIDTH
VMEM = pl.BlockSpec(memory_space=pltpu.VMEM)
HBM = pl.BlockSpec(memory_space=pltpu.HBM)
F32 = jnp.float32
BF16 = jnp.bfloat16


def call(body, outs, operands, in_hbm=False, mib=4, flops=0, nbytes=1 << 19, scratch=()):
    return pl.pallas_call(
        body,
        out_shape=[
            jax.ShapeDtypeStruct(s[:-1], BF16) if s[-1] is BF16 else jax.ShapeDtypeStruct(s, F32) for s in outs
        ],
        in_specs=[HBM if in_hbm else VMEM] * len(operands),
        out_specs=[VMEM] * len(outs),
        scratch_shapes=list(scratch),
        compiler_params=pltpu.CompilerParams(vmem_limit_bytes=mib << 20),
        cost_estimate=pl.CostEstimate(flops=flops, bytes_accessed=nbytes, transcendentals=0),
    )(*operands)


def core_of():
    return lax.rem(lax.axis_index("row"), 2)


def mask_body(*refs):
    sources, (own, sums, weights), targets, done = refs[:4], refs[4:7], refs[7:11], refs[11]
    copies = [pltpu.make_async_copy(a, b, done.at[i]) for i, (a, b) in enumerate(zip(sources, targets))]
    for copy in copies:
        copy.start()
    for copy in copies[1:]:
        copy.wait()
    panel, tile_mask, classes, class_weight = targets
    of = classes[...]
    found = jnp.zeros((1, PANEL), F32)
    for k in range(class_weight.shape[1]):
        found = jnp.where(of == k, class_weight[0, k], found)
    weights[...] = found
    copies[0].wait()
    for t in range(PANEL // TILE):
        at = pl.ds(t * TILE, TILE)
        kept = panel[:, at] * tile_mask[0, t].astype(F32)
        own[:, at] = kept
        sums[:, at] = jnp.broadcast_to(jnp.sum(kept, axis=0, keepdims=True), (8, TILE))


def join_body(own, other, chip, again):
    for out in (chip, again):
        out[pl.ds(0, WIDTH), :] = own[...]
        out[pl.ds(WIDTH, WIDTH), :] = other[...]


def add_body(a, b, out):
    out[...] = a[...] + b[...]


def put_body(a, b, panels, out, sums):
    sums[...] = a[...] + b[...]
    out[pl.ds(0, 2 * WIDTH), :] = panels[pl.ds(0, 2 * WIDTH), :]
    out[pl.ds(2 * WIDTH, 8), :] = sums[...]


def split(x):
    high = x.astype(BF16)
    return high, (x - high.astype(F32)).astype(BF16)


def dot3(ah, al, bh, bl):
    dims = (((1,), (1,)), ((), ()))
    dot = functools.partial(lax.dot_general, dimension_numbers=dims, preferred_element_type=F32)
    return dot(ah, bh) + (dot(ah, bl) + dot(al, bh))


def fill_rows(ph, pl_, weights, start, source, swapped):
    z, core = lax.axis_index("dom"), core_of()
    w = weights[...]
    first, second = (WIDTH, 0) if swapped else (0, WIDTH)
    for j in range(8):
        ahead = z + 8 - j
        behind = z if j == 0 else z + 8 + j
        at = lax.rem(jnp.where(core == 0, ahead, behind), N_DOM) * POS
        mine = source[pl.ds(pl.multiple_of(at + first, POS), POS), :]
        theirs = source[pl.ds(pl.multiple_of(at + second, POS), POS), :]
        to = pl.ds(start + j * 2 * POS, 2 * POS)
        ph[to, :], pl_[to, :] = split(jnp.concatenate([mine, theirs], axis=0) * w)


def fill_columns(qh, ql, start, source, swapped):
    for g in range(2):
        at, of = pl.ds(start + g * WIDTH, WIDTH), pl.ds((1 - g if swapped else g) * WIDTH, WIDTH)
        qh[at, :], ql[at, :] = split(source[of, :])


def early_body(chip, *refs):
    sent, swap, weights = refs[:2], refs[2:4], refs[4]
    outs, (ph, pl_, qh, ql) = refs[5:8], refs[8:]
    core = core_of()
    fill_rows(ph, pl_, weights, 0, chip, False)
    fill_columns(qh, ql, 0, chip, False)

    @pl.when(core == 0)
    def _():
        for i in range(2):
            fill_rows(ph, pl_, weights, (i + 1) * WIDTH, swap[i], True)
            fill_columns(qh, ql, (i + 1) * PAIR, sent[i], False)

    @pl.when(core == 1)
    def _():
        for i in range(2):
            fill_rows(ph, pl_, weights, (i + 1) * WIDTH, sent[i], False)
            fill_columns(qh, ql, (i + 1) * PAIR, swap[i], True)

    block = dot3(ph[...], pl_[...], qh[...], ql[...])
    for i in range(3):
        for j in range(8):
            rows = i * WIDTH + j * 2 * POS
            at = pl.ds((j // 3) * EARLY_ROWS + i * 2 * POS, 2 * POS)
            outs[j % 3][at, :] = block[rows : rows + 2 * POS]


def late_body(sent, swap, weights, ph, pl_, qh, ql, sums, first, second, third, fh, fl, gh, gl):
    core = core_of()

    @pl.when(core == 0)
    def _():
        fill_rows(fh, fl, weights, 0, swap, True)
        fill_columns(gh, gl, 0, sent, False)

    @pl.when(core == 1)
    def _():
        fill_rows(fh, fl, weights, 0, sent, False)
        fill_columns(gh, gl, 0, swap, True)

    total = (sums[...] + swap[pl.ds(2 * WIDTH, 8), :]) * weights[...]
    at = pl.ds(WIDTH, 16)
    fh[at, :], fl[at, :] = split(jnp.concatenate([total, total], axis=0))
    late_early = dot3(fh[...], fl[...], qh[...], ql[...])
    late_late = dot3(fh[...], fl[...], gh[...], gl[...])
    early_late = dot3(ph[...], pl_[...], gh[...], gl[...])
    for j in range(8):
        out, start = (first, second, third)[j % 3], (j // 3) * LATE_ROWS
        rows = slice(j * 2 * POS, (j + 1) * 2 * POS)
        out[pl.ds(start, 2 * POS), :] = late_early[rows, : 2 * PAIR]
        at = pl.ds(start + 2 * POS, 2 * POS)
        out[at, pl.ds(0, PAIR)] = late_early[rows, 2 * PAIR :]
        out[at, pl.ds(PAIR, PAIR)] = late_late[rows]
        for i in range(3):
            for g in range(2):
                begin = i * WIDTH + j * 2 * POS + g * POS
                at = pl.ds(start + 4 * POS + i * POS, POS)
                out[at, pl.ds(g * PAIR, PAIR)] = early_late[begin : begin + POS]
    head = late_early[WIDTH : WIDTH + 8, : 2 * PAIR]
    tail = jnp.concatenate([late_early[WIDTH : WIDTH + 8, 2 * PAIR :], late_late[WIDTH : WIDTH + 8]], axis=1)
    odd = lax.broadcasted_iota(jnp.int32, (TOTALS, LATE_COLS), 0) % 2 == 1
    share = jnp.where(odd, tail, head)
    first[pl.ds(3 * LATE_ROWS, TOTALS), :] = share
    second[pl.ds(3 * LATE_ROWS, TOTALS), :] = share


def second_body(u, r, out, unit):
    far = (core_of() == 0).astype(F32)
    head, tail = pl.ds(0, unit), pl.ds(unit, u.shape[0] - unit)
    out[head, :] = u[head, :] + r[head, :] * far
    out[tail, :] = u[tail, :] + r[tail, :]


def third_body(u2, r2, *refs, unit):
    out = refs[-1]
    out[pl.ds(0, unit), :] = u2[pl.ds(0, unit), :] + r2[pl.ds(0, unit), :]
    if len(refs) == 3:
        u1, s2 = refs[:2]
        at = pl.ds(3 * unit, TOTALS)
        wide = u1[at, :] + r2[at, :]
        narrow = (lax.broadcasted_iota(jnp.int32, wide.shape, 0) >= 2) & (core_of() == 1)
        out[pl.ds(unit, TOTALS), :] = jnp.where(narrow, s2[at, :], wide)


def fourth_body(u2, r2, r3, out, unit):
    at = pl.ds(unit, unit)
    out[pl.ds(0, unit), :] = u2[at, :] + r2[at, :] + r3[pl.ds(0, unit), :]
    if out.shape[0] > unit:
        out[pl.ds(unit, TOTALS), :] = r3[pl.ds(unit, TOTALS), :]


def give_body(u0a, r2a, r4a, u0b, r2b, r3b, r4b, give, keep):
    late = (core_of() == 1).astype(F32)

    def early(start, to):
        at, of = pl.ds(start, POS), pl.ds(2 * EARLY_ROWS + start, POS)
        return r2a[of, to] + u0a[at, to] * late + r4a[at, to]

    def other(start, to):
        at, of = pl.ds(start, POS), pl.ds(2 * LATE_ROWS + start, POS)
        return r2b[of, to] + u0b[at, to] * late + r4b[at, to]

    def pairs(k, count=1):
        return pl.ds(k * PAIR, count * PAIR)

    for g, out in enumerate((keep, give)):
        for n in range(3):
            at = pl.ds(n * POS, POS)
            out[at, pairs(0, 3)] = early(n * 2 * POS + g * POS, pairs(0, 3))
            out[at, pairs(3)] = other(4 * POS + n * POS, pairs(g))
        at = pl.ds(3 * POS, POS)
        out[at, pairs(0, 2)] = other(g * POS, pairs(0, 2))
        out[at, pairs(2, 2)] = other(2 * POS + g * POS, pairs(0, 2))
    at = pl.ds(3 * LATE_ROWS, TOTALS)
    sums = r2b[at, :] + u0b[at, :] * late
    for k in range(2):
        total = sums[k : k + 1] + r3b[pl.ds(LATE_ROWS + k, 1), :] + r4b[pl.ds(LATE_ROWS + 2 + k, 1), :]
        for out in (keep, give):
            out[pl.ds(PART, 1), pairs(2 * k, 2)] = total


def finish_body(keep, here, out):
    x, r, z = lax.axis_index("col"), lax.axis_index("row"), lax.axis_index("dom")
    core = lax.rem(r, 2)
    y = lax.div(r, 2)
    lanes = lax.broadcasted_iota(jnp.int32, (POS, WIDTH), 1)
    rows = lax.broadcasted_iota(jnp.int32, (POS, WIDTH), 0)
    unit = (lanes == z * POS + rows).astype(F32)
    for m in range(4):
        for g in range(2):
            mine, theirs = pl.ds(m * PAIR + g * WIDTH, WIDTH), pl.ds(m * PAIR + (1 - g) * WIDTH, WIDTH)
            total = keep[pl.ds(PART, 1), mine] + here[pl.ds(PART, 1), theirs]
            scale = PROT / (total + 1.0)
            group = 2 * lax.rem(y + m, 4) + (core if g == 0 else 1 - core)
            for n in range(N_COL):
                at = pl.ds(n * POS, POS)
                block = keep[at, mine] + here[at, theirs]
                if n == 0 and m == 0 and g == 0:
                    block = block + unit
                place = lax.rem(x + n, N_COL) * (POS * N_ROW) + group
                out[pl.ds(place, POS, stride=N_ROW), :] = block * scale


def across(a):
    return lax.ppermute(a, "row", [(i, i ^ 1) for i in range(N_ROW)])


def around(a, shift):
    pairs = []
    for r in range(N_ROW):
        for c in range(N_COL):
            to = ((r + 2 * shift) % N_ROW, c) if r % 2 == 0 else (r, (c + shift) % N_COL)
            pairs.append((r * N_COL + c, to[0] * N_COL + to[1]))
    return lax.ppermute(a, ("row", "col"), pairs)


def doubled(a, bit):
    pairs = []
    for r in range(N_ROW):
        for c in range(N_COL):
            to = (r, c ^ bit) if r % 2 == 0 else (r ^ (2 * bit), c)
            pairs.append((r * N_COL + c, to[0] * N_COL + to[1]))
    return lax.ppermute(a, ("row", "col"), pairs)


def after(a, *done):
    return lax.optimization_barrier((a, *done))[0]


def along_z(a, shift):
    pairs = []
    for z in range(N_DOM):
        for r in range(N_ROW):
            to = (z + (shift if r % 2 == 0 else -shift)) % N_DOM
            pairs.append((z * N_ROW + r, to * N_ROW + r))
    return lax.ppermute(a, ("dom", "row"), pairs)


def per_device(protein_panel, tile_mask, domain_class, class_weight):
    tiles, classes = PANEL // TILE, class_weight.shape[0]
    own, sums, weights = call(
        mask_body,
        [(WIDTH, PANEL), (8, PANEL), (1, PANEL)],
        [
            protein_panel.reshape(WIDTH, PANEL),
            tile_mask.reshape(1, tiles),
            domain_class.reshape(1, PANEL),
            class_weight.reshape(1, classes),
        ],
        in_hbm=True, mib=4,
        scratch=[
            pltpu.VMEM((WIDTH, PANEL), F32),
            pltpu.SMEM((1, tiles), jnp.int32),
            pltpu.VMEM((1, PANEL), jnp.int32),
            pltpu.SMEM((1, classes), F32),
            pltpu.SemaphoreType.DMA((4,)),
        ],
    )
    other = across(own)
    chip, again = call(join_body, [(2 * WIDTH, PANEL), (2 * WIDTH + 24, PANEL)], [own, other])
    from_next, from_far, from_last = around(chip, -1), around(chip, 2), around(again, 1)

    def both(a, bit):
        return call(add_body, [(8, PANEL)], [a, doubled(a, bit)])[0]

    sums = both(both(sums, 1), 2)
    swap_next = across(after(from_next, sums))
    sums = across(sums)
    swap_far = across(after(from_far, sums))
    sums = both(sums, 1)
    early, columns = (3 * WIDTH, PANEL, BF16), (EARLY_COLS, PANEL, BF16)
    a0, a1, a2, ph, pl_, qh, ql = call(
        early_body,
        [(k * EARLY_ROWS, EARLY_COLS) for k in (3, 3, 2)] + [early, early, columns, columns],
        [chip, from_next, from_far, swap_next, swap_far, weights],
        mib=16, nbytes=8 << 20,
    )
    ar1 = along_z(a0, 1)
    from_last, sums = call(put_body, [(2 * WIDTH + 8, PANEL), (8, PANEL)], [sums, doubled(sums, 2), after(from_last, a0)])
    swap_last = across(from_last)
    b0, b1, b2 = call(
        late_body,
        [(3 * LATE_ROWS + TOTALS, LATE_COLS), (3 * LATE_ROWS + TOTALS, LATE_COLS), (2 * LATE_ROWS, LATE_COLS)],
        [from_last, swap_last, weights, ph, pl_, qh, ql, sums],
        mib=16, nbytes=0,
        scratch=[pltpu.VMEM((WIDTH + 16, PANEL), BF16)] * 2 + [pltpu.VMEM((PAIR, PANEL), BF16)] * 2,
    )
    br1 = along_z(b0, 1)
    of_a, of_b = {"unit": EARLY_ROWS}, {"unit": LATE_ROWS}
    with_unit = functools.partial
    (as2,) = call(with_unit(second_body, **of_a), [a1.shape], [a1, ar1])
    ar2 = along_z(as2, 1)
    (bs2,) = call(with_unit(second_body, **of_b), [b1.shape], [b1, br1])
    br2 = along_z(bs2, 1)
    (as3,) = call(with_unit(third_body, **of_a), [(EARLY_ROWS, EARLY_COLS)], [a2, ar2])
    ar3 = along_z(as3, 3)
    (bs3,) = call(with_unit(third_body, **of_b), [(LATE_ROWS + TOTALS, LATE_COLS)], [b2, br2, b1, bs2])
    br3 = along_z(bs3, 3)
    (as4,) = call(with_unit(fourth_body, **of_a), [(EARLY_ROWS, EARLY_COLS)], [a2, ar2, ar3])
    ar4 = along_z(as4, 3)
    (bs4,) = call(with_unit(fourth_body, **of_b), [(LATE_ROWS + TOTALS, LATE_COLS)], [b2, br2, br3])
    br4 = along_z(bs4, 3)
    give, keep = call(give_body, [(PART + TOTALS, 4 * PAIR)] * 2, [a0, ar2, ar4, b0, br2, br3, br4])
    (flow,) = call(finish_body, [(N_COL * POS * N_ROW, WIDTH)], [keep, across(give)])
    return flow.reshape(1, N_COL, POS, N_ROW, 1, WIDTH)


def solution(mesh):
    placed = (P("row", "col", None, "dom"), P("row", "col", None, "dom"), P("dom"), P())
    return jax.shard_map(
        per_device,
        mesh=mesh,
        in_specs=placed,
        out_specs=P("row", None, "dom", None, "col", None),
        check_vma=False,
    )
```

```python
import functools

import jax
import jax.numpy as jnp
from jax import lax
from jax.experimental import pallas as pl
from jax.experimental.pallas import tpu as pltpu
from jax.sharding import PartitionSpec as P

TILE = 128
N_DOM, N_ROW, N_COL = 16, 8, 4
WIDTH = 128
PANEL = 1024
POS = WIDTH // N_DOM
PAIR = 2 * WIDTH
EARLY_ROWS, EARLY_COLS = 3 * 2 * POS, 3 * PAIR
LATE_ROWS, LATE_COLS = 2 * 2 * POS + 3 * POS, 2 * PAIR
TOTALS = 8
PART = N_COL * POS
ORDER = (7, 3, 5, 1, 6, 2, 4, 0)
PROT = N_ROW * N_COL * WIDTH
VMEM = pl.BlockSpec(memory_space=pltpu.VMEM)
HBM = pl.BlockSpec(memory_space=pltpu.HBM)
F32 = jnp.float32
BF16 = jnp.bfloat16


def call(body, outs, operands, in_hbm=(), mib=4, flops=0, nbytes=1 << 19, scratch=()):
    return pl.pallas_call(
        body,
        out_shape=[
            jax.ShapeDtypeStruct(s[:-1], BF16) if s[-1] is BF16 else jax.ShapeDtypeStruct(s, F32) for s in outs
        ],
        in_specs=[HBM if i in in_hbm else VMEM for i in range(len(operands))],
        out_specs=[VMEM] * len(outs),
        scratch_shapes=list(scratch),
        compiler_params=pltpu.CompilerParams(vmem_limit_bytes=mib << 20),
        cost_estimate=pl.CostEstimate(flops=flops, bytes_accessed=nbytes, transcendentals=0),
    )(*operands)


def core_of():
    return lax.rem(lax.axis_index("row"), 2)


def mask_body(*refs):
    sources, (own, sums, weights), targets, done = refs[:4], refs[4:7], refs[7:11], refs[11]
    copies = [pltpu.make_async_copy(a, b, done.at[i]) for i, (a, b) in enumerate(zip(sources, targets))]
    for copy in copies:
        copy.start()
    for copy in copies[1:]:
        copy.wait()
    panel, tile_mask, classes, class_weight = targets
    of = classes[...]
    found = jnp.zeros((1, PANEL), F32)
    for k in range(class_weight.shape[1]):
        found = jnp.where(of == k, class_weight[0, k], found)
    weights[...] = found
    copies[0].wait()
    for t in range(PANEL // TILE):
        at = pl.ds(t * TILE, TILE)
        kept = panel[:, at] * tile_mask[0, t].astype(F32)
        own[:, at] = kept
        sums[:, at] = jnp.broadcast_to(jnp.sum(kept, axis=0, keepdims=True), (8, TILE))


def join_body(own, other, chip, again):
    for out in (chip, again):
        out[pl.ds(0, WIDTH), :] = own[...]
        out[pl.ds(WIDTH, WIDTH), :] = other[...]


def add_body(a, b, out):
    out[...] = a[...] + b[...]


def put_body(a, b, panels, out, sums):
    sums[...] = a[...] + b[...]
    out[pl.ds(0, 2 * WIDTH), :] = panels[pl.ds(0, 2 * WIDTH), :]
    out[pl.ds(2 * WIDTH, 8), :] = sums[...]


def split(x):
    high = x.astype(BF16)
    return high, (x - high.astype(F32)).astype(BF16)


def dot3(ah, al, bh, bl):
    dims = (((1,), (1,)), ((), ()))
    dot = functools.partial(lax.dot_general, dimension_numbers=dims, preferred_element_type=F32)
    return dot(ah, bh) + (dot(ah, bl) + dot(al, bh))


def fill_rows(ph, pl_, weights, start, source, swapped):
    z, core = lax.axis_index("dom"), core_of()
    w = weights[...]
    first, second = (WIDTH, 0) if swapped else (0, WIDTH)
    for j, far in enumerate(ORDER):
        at = lax.rem(jnp.where(core == 0, z + far, z + N_DOM - 1 - far), N_DOM) * POS
        mine = source[pl.ds(pl.multiple_of(at + first, POS), POS), :]
        theirs = source[pl.ds(pl.multiple_of(at + second, POS), POS), :]
        to = pl.ds(start + j * 2 * POS, 2 * POS)
        ph[to, :], pl_[to, :] = split(jnp.concatenate([mine, theirs], axis=0) * w)


def fill_columns(qh, ql, start, source, swapped):
    for g in range(2):
        at, of = pl.ds(start + g * WIDTH, WIDTH), pl.ds((1 - g if swapped else g) * WIDTH, WIDTH)
        qh[at, :], ql[at, :] = split(source[of, :])


def early_body(chip, *refs):
    sent, swap, weights = refs[:2], refs[2:4], refs[4]
    outs, (ph, pl_, qh, ql) = refs[5:7], refs[7:]
    core = core_of()
    fill_rows(ph, pl_, weights, 0, chip, False)
    fill_columns(qh, ql, 0, chip, False)

    @pl.when(core == 0)
    def _():
        for i in range(2):
            fill_rows(ph, pl_, weights, (i + 1) * WIDTH, swap[i], True)
            fill_columns(qh, ql, (i + 1) * PAIR, sent[i], False)

    @pl.when(core == 1)
    def _():
        for i in range(2):
            fill_rows(ph, pl_, weights, (i + 1) * WIDTH, sent[i], False)
            fill_columns(qh, ql, (i + 1) * PAIR, swap[i], True)

    block = dot3(ph[...], pl_[...], qh[...], ql[...])
    for i in range(3):
        for j in range(8):
            rows = i * WIDTH + j * 2 * POS
            at = pl.ds((j % 4) * EARLY_ROWS + i * 2 * POS, 2 * POS)
            outs[j // 4][at, :] = block[rows : rows + 2 * POS]


def late_body(sent, swap, weights, ph, pl_, qh, ql, sums, first, second, fh, fl, gh, gl):
    core = core_of()

    @pl.when(core == 0)
    def _():
        fill_rows(fh, fl, weights, 0, swap, True)
        fill_columns(gh, gl, 0, sent, False)

    @pl.when(core == 1)
    def _():
        fill_rows(fh, fl, weights, 0, sent, False)
        fill_columns(gh, gl, 0, swap, True)

    total = (sums[...] + swap[pl.ds(2 * WIDTH, 8), :]) * weights[...]
    at = pl.ds(WIDTH, 16)
    fh[at, :], fl[at, :] = split(jnp.concatenate([total, total], axis=0))
    late_early = dot3(fh[...], fl[...], qh[...], ql[...])
    late_late = dot3(fh[...], fl[...], gh[...], gl[...])
    early_late = dot3(ph[...], pl_[...], gh[...], gl[...])
    for j in range(8):
        out, start = (first, second)[j // 4], (j % 4) * LATE_ROWS
        rows = slice(j * 2 * POS, (j + 1) * 2 * POS)
        out[pl.ds(start, 2 * POS), :] = late_early[rows, : 2 * PAIR]
        at = pl.ds(start + 2 * POS, 2 * POS)
        out[at, pl.ds(0, PAIR)] = late_early[rows, 2 * PAIR :]
        out[at, pl.ds(PAIR, PAIR)] = late_late[rows]
        for i in range(3):
            for g in range(2):
                begin = i * WIDTH + j * 2 * POS + g * POS
                at = pl.ds(start + 4 * POS + i * POS, POS)
                out[at, pl.ds(g * PAIR, PAIR)] = early_late[begin : begin + POS]
    head = late_early[WIDTH : WIDTH + 8, : 2 * PAIR]
    tail = jnp.concatenate([late_early[WIDTH : WIDTH + 8, 2 * PAIR :], late_late[WIDTH : WIDTH + 8]], axis=1)
    odd = lax.broadcasted_iota(jnp.int32, (TOTALS, LATE_COLS), 0) % 2 == 1
    share = jnp.where(odd, tail, head)
    first[pl.ds(4 * LATE_ROWS, TOTALS), :] = share
    second[pl.ds(4 * LATE_ROWS, TOTALS), :] = share


def step_body(mine, came, go, stay, half):
    go[pl.ds(0, half), :] = mine[pl.ds(0, half), :] + came[pl.ds(0, half), :]
    stay[pl.ds(0, half), :] = mine[pl.ds(half, half), :] + came[pl.ds(half, half), :]
    if half < go.shape[0]:
        at = pl.ds(2 * half, TOTALS)
        both = mine[at, :] + came[at, :]
        go[pl.ds(half, TOTALS), :] = both
        stay[pl.ds(half, TOTALS), :] = both


def give_body(mine_a, came_a, mine_b, came_b, give, keep):
    def early(start, to):
        return mine_a[pl.ds(start, POS), to] + came_a[pl.ds(start, POS), to]

    def other(start, to):
        return mine_b[pl.ds(start, POS), to] + came_b[pl.ds(start, POS), to]

    def pairs(k, count=1):
        return pl.ds(k * PAIR, count * PAIR)

    for g, out in enumerate((keep, give)):
        for n in range(3):
            at = pl.ds(n * POS, POS)
            out[at, pairs(0, 3)] = early(n * 2 * POS + g * POS, pairs(0, 3))
            out[at, pairs(3)] = other(4 * POS + n * POS, pairs(g))
        at = pl.ds(3 * POS, POS)
        out[at, pairs(0, 2)] = other(g * POS, pairs(0, 2))
        out[at, pairs(2, 2)] = other(2 * POS + g * POS, pairs(0, 2))
    for k in range(2):
        at = pl.ds(LATE_ROWS + k, 1)
        total = mine_b[at, :] + came_b[at, :]
        for out in (keep, give):
            out[pl.ds(PART, 1), pairs(2 * k, 2)] = total


def finish_body(keep, here, out):
    x, r, z = lax.axis_index("col"), lax.axis_index("row"), lax.axis_index("dom")
    core = lax.rem(r, 2)
    y = lax.div(r, 2)
    lanes = lax.broadcasted_iota(jnp.int32, (POS, WIDTH), 1)
    rows = lax.broadcasted_iota(jnp.int32, (POS, WIDTH), 0)
    unit = (lanes == z * POS + rows).astype(F32)
    for m in range(4):
        for g in range(2):
            mine, theirs = pl.ds(m * PAIR + g * WIDTH, WIDTH), pl.ds(m * PAIR + (1 - g) * WIDTH, WIDTH)
            total = keep[pl.ds(PART, 1), mine] + here[pl.ds(PART, 1), theirs]
            scale = PROT / (total + 1.0)
            group = 2 * lax.rem(y + m, 4) + (core if g == 0 else 1 - core)
            for n in range(N_COL):
                at = pl.ds(n * POS, POS)
                block = keep[at, mine] + here[at, theirs]
                if n == 0 and m == 0 and g == 0:
                    block = block + unit
                place = lax.rem(x + n, N_COL) * (POS * N_ROW) + group
                out[pl.ds(place, POS, stride=N_ROW), :] = block * scale


def across(a):
    return lax.ppermute(a, "row", [(i, i ^ 1) for i in range(N_ROW)])


def around(a, shift):
    pairs = []
    for r in range(N_ROW):
        for c in range(N_COL):
            to = ((r + 2 * shift) % N_ROW, c) if r % 2 == 0 else (r, (c + shift) % N_COL)
            pairs.append((r * N_COL + c, to[0] * N_COL + to[1]))
    return lax.ppermute(a, ("row", "col"), pairs)


def doubled(a, bit):
    pairs = []
    for r in range(N_ROW):
        for c in range(N_COL):
            to = (r, c ^ bit) if r % 2 == 0 else (r ^ (2 * bit), c)
            pairs.append((r * N_COL + c, to[0] * N_COL + to[1]))
    return lax.ppermute(a, ("row", "col"), pairs)


def after(a, *done):
    return lax.optimization_barrier((a, *done))[0]


def along_z(a, shift):
    pairs = []
    for z in range(N_DOM):
        for r in range(N_ROW):
            to = (z + (shift if r % 2 == 0 else -shift)) % N_DOM
            pairs.append((z * N_ROW + r, to * N_ROW + r))
    return lax.ppermute(a, ("dom", "row"), pairs)


def settled(a, cross):
    pairs = []
    for z in range(N_DOM):
        for r in range(N_ROW):
            to = z if r % 2 == 0 else (z - 1) % N_DOM
            pairs.append((z * N_ROW + r, to * N_ROW + (r ^ cross)))
    return lax.ppermute(a, ("dom", "row"), pairs)


def per_device(protein_panel, tile_mask, domain_class, class_weight):
    tiles, classes = PANEL // TILE, class_weight.shape[0]
    own, sums, weights = call(
        mask_body,
        [(WIDTH, PANEL), (8, PANEL), (1, PANEL)],
        [
            protein_panel.reshape(WIDTH, PANEL),
            tile_mask.reshape(1, tiles),
            domain_class.reshape(1, PANEL),
            class_weight.reshape(1, classes),
        ],
        in_hbm=range(4),
        scratch=[
            pltpu.VMEM((WIDTH, PANEL), F32),
            pltpu.SMEM((1, tiles), jnp.int32),
            pltpu.VMEM((1, PANEL), jnp.int32),
            pltpu.SMEM((1, classes), F32),
            pltpu.SemaphoreType.DMA((4,)),
        ],
    )
    other = across(own)
    chip, again = call(join_body, [(2 * WIDTH, PANEL), (2 * WIDTH + 24, PANEL)], [own, other])
    from_next, from_far, from_last = around(chip, -1), around(chip, 2), around(again, 1)

    def both(a, bit):
        return call(add_body, [(8, PANEL)], [a, doubled(a, bit)])[0]

    sums = across(both(both(sums, 1), 2))
    swap_far = across(after(from_far, sums))
    sums = both(sums, 1)
    swap_next = across(after(from_next, sums))
    early, columns = (3 * WIDTH, PANEL, BF16), (EARLY_COLS, PANEL, BF16)
    a0, a1, ph, pl_, qh, ql = call(
        early_body,
        [(4 * EARLY_ROWS, EARLY_COLS)] * 2 + [early, early, columns, columns],
        [chip, from_next, from_far, swap_next, swap_far, weights],
        mib=16, nbytes=8 << 20,
    )
    came_a = along_z(a0, 1)
    from_last, sums = call(put_body, [(2 * WIDTH + 8, PANEL), (8, PANEL)], [sums, doubled(sums, 2), after(from_last, a0)])
    swap_last = across(from_last)
    b0, b1 = call(
        late_body,
        [(4 * LATE_ROWS + TOTALS, LATE_COLS)] * 2,
        [from_last, swap_last, weights, ph, pl_, qh, ql, sums],
        mib=16, nbytes=0,
        scratch=[pltpu.VMEM((WIDTH + 16, PANEL), BF16)] * 2 + [pltpu.VMEM((PAIR, PANEL), BF16)] * 2,
    )
    came_b = along_z(b0, 1)

    def step(mine, came, rows, totals, shift):
        shape = (rows + totals, mine.shape[1])
        go, stay = call(functools.partial(step_body, half=rows), [shape] * 2, [mine, came])
        return stay, along_z(go, shift)

    a1, came_a = step(a1, came_a, 2 * EARLY_ROWS, 0, 2)
    b1, came_b = step(b1, came_b, 2 * LATE_ROWS, TOTALS, 2)
    a1, came_a = step(a1, came_a, EARLY_ROWS, 0, 4)
    b1, came_b = step(b1, came_b, LATE_ROWS, TOTALS, 4)
    give, keep = call(give_body, [(PART + TOTALS, 4 * PAIR)] * 2, [a1, came_a, b1, came_b])
    (flow,) = call(finish_body, [(N_COL * POS * N_ROW, WIDTH)], [settled(keep, 0), settled(give, 1)])
    return flow.reshape(1, N_COL, POS, N_ROW, 1, WIDTH)


def solution(mesh):
    placed = (P("row", "col", None, "dom"), P("row", "col", None, "dom"), P("dom"), P())
    return jax.shard_map(
        per_device,
        mesh=mesh,
        in_specs=placed,
        out_specs=P("row", None, "dom", None, "col", None),
        check_vma=False,
    )
```

```python
import functools

import jax
import jax.numpy as jnp
from jax import lax
from jax.experimental import pallas as pl
from jax.experimental.pallas import tpu as pltpu
from jax.sharding import PartitionSpec as P

TILE = 128
N_DOM, N_ROW, N_COL = 16, 8, 4
WIDTH = 128
PANEL = 1024
POS = WIDTH // N_DOM
PAIR = 2 * WIDTH
EARLY_ROWS, EARLY_COLS = 3 * 2 * POS, 3 * PAIR
LATE_ROWS, LATE_COLS = 2 * 2 * POS + 3 * POS, 2 * PAIR
TOTALS = 8
PART = N_COL * POS
ORDER = (7, 3, 5, 1, 6, 2, 4, 0)
PROT = N_ROW * N_COL * WIDTH
VMEM = pl.BlockSpec(memory_space=pltpu.VMEM)
HBM = pl.BlockSpec(memory_space=pltpu.HBM)
F32 = jnp.float32
BF16 = jnp.bfloat16


def call(body, outs, operands, in_hbm=(), mib=4, flops=0, nbytes=1 << 19, scratch=()):
    return pl.pallas_call(
        body,
        out_shape=[
            jax.ShapeDtypeStruct(s[:-1], BF16) if s[-1] is BF16 else jax.ShapeDtypeStruct(s, F32) for s in outs
        ],
        in_specs=[HBM if i in in_hbm else VMEM for i in range(len(operands))],
        out_specs=[VMEM] * len(outs),
        scratch_shapes=list(scratch),
        compiler_params=pltpu.CompilerParams(vmem_limit_bytes=mib << 20),
        cost_estimate=pl.CostEstimate(flops=flops, bytes_accessed=nbytes, transcendentals=0),
    )(*operands)


def core_of():
    return lax.rem(lax.axis_index("row"), 2)


def mask_body(*refs):
    sources, (own, sums, weights), targets, done = refs[:4], refs[4:7], refs[7:11], refs[11]
    copies = [pltpu.make_async_copy(a, b, done.at[i]) for i, (a, b) in enumerate(zip(sources, targets))]
    for copy in copies:
        copy.start()
    for copy in copies[1:]:
        copy.wait()
    panel, tile_mask, classes, class_weight = targets
    of = classes[...]
    found = jnp.zeros((1, PANEL), F32)
    for k in range(class_weight.shape[1]):
        found = jnp.where(of == k, class_weight[0, k], found)
    weights[...] = found
    copies[0].wait()
    for t in range(PANEL // TILE):
        at = pl.ds(t * TILE, TILE)
        kept = panel[:, at] * tile_mask[0, t].astype(F32)
        own[:, at] = kept
        sums[:, at] = jnp.broadcast_to(jnp.sum(kept, axis=0, keepdims=True), (8, TILE))


def join_body(own, other, chip, again):
    for out in (chip, again):
        out[pl.ds(0, WIDTH), :] = own[...]
        out[pl.ds(WIDTH, WIDTH), :] = other[...]


def add_body(a, b, out):
    out[...] = a[...] + b[...]


def put_body(a, b, panels, out, sums):
    sums[...] = a[...] + b[...]
    out[pl.ds(0, 2 * WIDTH), :] = panels[pl.ds(0, 2 * WIDTH), :]
    out[pl.ds(2 * WIDTH, 8), :] = sums[...]


def split(x):
    high = x.astype(BF16)
    return high, (x - high.astype(F32)).astype(BF16)


def dot3(ah, al, bh, bl):
    dims = (((1,), (1,)), ((), ()))
    dot = functools.partial(lax.dot_general, dimension_numbers=dims, preferred_element_type=F32)
    return dot(ah, bh) + (dot(ah, bl) + dot(al, bh))


def fill_rows(ph, pl_, weights, start, source, swapped):
    z, core = lax.axis_index("dom"), core_of()
    w = weights[...]
    first, second = (WIDTH, 0) if swapped else (0, WIDTH)
    for j, far in enumerate(ORDER):
        at = lax.rem(jnp.where(core == 0, z + far, z + N_DOM - 1 - far), N_DOM) * POS
        mine = source[pl.ds(pl.multiple_of(at + first, POS), POS), :]
        theirs = source[pl.ds(pl.multiple_of(at + second, POS), POS), :]
        to = pl.ds(start + j * 2 * POS, 2 * POS)
        ph[to, :], pl_[to, :] = split(jnp.concatenate([mine, theirs], axis=0) * w)


def fill_columns(qh, ql, start, source, swapped):
    for g in range(2):
        at, of = pl.ds(start + g * WIDTH, WIDTH), pl.ds((1 - g if swapped else g) * WIDTH, WIDTH)
        qh[at, :], ql[at, :] = split(source[of, :])


def early_body(chip, *refs):
    sent, swap, weights = refs[:2], refs[2:4], refs[4]
    outs, (ph, pl_, qh, ql) = refs[5:7], refs[7:]
    core = core_of()
    fill_rows(ph, pl_, weights, 0, chip, False)
    fill_columns(qh, ql, 0, chip, False)

    @pl.when(core == 0)
    def _():
        for i in range(2):
            fill_rows(ph, pl_, weights, (i + 1) * WIDTH, swap[i], True)
            fill_columns(qh, ql, (i + 1) * PAIR, sent[i], False)

    @pl.when(core == 1)
    def _():
        for i in range(2):
            fill_rows(ph, pl_, weights, (i + 1) * WIDTH, sent[i], False)
            fill_columns(qh, ql, (i + 1) * PAIR, swap[i], True)

    block = dot3(ph[...], pl_[...], qh[...], ql[...])
    for i in range(3):
        for j in range(8):
            rows = i * WIDTH + j * 2 * POS
            at = pl.ds((j % 4) * EARLY_ROWS + i * 2 * POS, 2 * POS)
            outs[j // 4][at, :] = block[rows : rows + 2 * POS]


def late_body(sent, swap, weights, ph, pl_, qh, ql, sums, first, second, fh, fl, gh, gl):
    core = core_of()

    @pl.when(core == 0)
    def _():
        fill_rows(fh, fl, weights, 0, swap, True)
        fill_columns(gh, gl, 0, sent, False)

    @pl.when(core == 1)
    def _():
        fill_rows(fh, fl, weights, 0, sent, False)
        fill_columns(gh, gl, 0, swap, True)

    total = (sums[...] + swap[pl.ds(2 * WIDTH, 8), :]) * weights[...]
    at = pl.ds(WIDTH, 16)
    fh[at, :], fl[at, :] = split(jnp.concatenate([total, total], axis=0))
    late_early = dot3(fh[...], fl[...], qh[...], ql[...])
    late_late = dot3(fh[...], fl[...], gh[...], gl[...])
    early_late = dot3(ph[...], pl_[...], gh[...], gl[...])
    for j in range(8):
        out, start = (first, second)[j // 4], (j % 4) * LATE_ROWS
        rows = slice(j * 2 * POS, (j + 1) * 2 * POS)
        out[pl.ds(start, 2 * POS), :] = late_early[rows, : 2 * PAIR]
        at = pl.ds(start + 2 * POS, 2 * POS)
        out[at, pl.ds(0, PAIR)] = late_early[rows, 2 * PAIR :]
        out[at, pl.ds(PAIR, PAIR)] = late_late[rows]
        for i in range(3):
            for g in range(2):
                begin = i * WIDTH + j * 2 * POS + g * POS
                at = pl.ds(start + 4 * POS + i * POS, POS)
                out[at, pl.ds(g * PAIR, PAIR)] = early_late[begin : begin + POS]
    head = late_early[WIDTH : WIDTH + 8, : 2 * PAIR]
    tail = jnp.concatenate([late_early[WIDTH : WIDTH + 8, 2 * PAIR :], late_late[WIDTH : WIDTH + 8]], axis=1)
    odd = lax.broadcasted_iota(jnp.int32, (TOTALS, LATE_COLS), 0) % 2 == 1
    share = jnp.where(odd, tail, head)
    first[pl.ds(4 * LATE_ROWS, TOTALS), :] = share
    second[pl.ds(4 * LATE_ROWS, TOTALS), :] = share


def step_body(mine, came, go, stay, half):
    go[pl.ds(0, half), :] = mine[pl.ds(0, half), :] + came[pl.ds(0, half), :]
    stay[pl.ds(0, half), :] = mine[pl.ds(half, half), :] + came[pl.ds(half, half), :]
    if half < go.shape[0]:
        at = pl.ds(2 * half, TOTALS)
        both = mine[at, :] + came[at, :]
        go[pl.ds(half, TOTALS), :] = both
        stay[pl.ds(half, TOTALS), :] = both


def give_early_body(mine, came, give, keep):
    for g, out in enumerate((keep, give)):
        for n in range(3):
            at = pl.ds(n * 2 * POS + g * POS, POS)
            out[pl.ds(n * POS, POS), :] = mine[at, :] + came[at, :]


def give_late_body(mine, came, give, keep):
    for g, out in enumerate((keep, give)):
        for k in range(2):
            at = pl.ds(k * 2 * POS + g * POS, POS)
            out[pl.ds(k * POS, POS), :] = mine[at, :] + came[at, :]
        for n in range(3):
            at, to = pl.ds(4 * POS + n * POS, POS), pl.ds(g * PAIR, PAIR)
            out[pl.ds((2 + n) * POS, POS), pl.ds(0, PAIR)] = mine[at, to] + came[at, to]
        out[pl.ds(2 * POS, 3 * POS), pl.ds(PAIR, PAIR)] = jnp.zeros((3 * POS, PAIR), F32)
        at = pl.ds(LATE_ROWS, TOTALS)
        out[pl.ds(5 * POS, TOTALS), :] = mine[at, :] + came[at, :]


def finish_body(keep_a, here_a, keep_b, here_b, out):
    x, r, z = lax.axis_index("col"), lax.axis_index("row"), lax.axis_index("dom")
    core = lax.rem(r, 2)
    y = lax.div(r, 2)
    lanes = lax.broadcasted_iota(jnp.int32, (POS, WIDTH), 1)
    rows = lax.broadcasted_iota(jnp.int32, (POS, WIDTH), 0)
    unit = (lanes == z * POS + rows).astype(F32)
    for m in range(4):
        for g in range(2):
            mine, theirs = m * PAIR + g * WIDTH, m * PAIR + (1 - g) * WIDTH

            def folded(ref, row, lane):
                return ref[row, pl.ds(lane % LATE_COLS, WIDTH)]

            at = pl.ds(5 * POS + m // 2, 1)
            total = folded(keep_b, at, mine) + folded(here_b, at, theirs)
            scale = PROT / (total + 1.0)
            group = 2 * lax.rem(y + m, 4) + (core if g == 0 else 1 - core)
            for n in range(N_COL):
                if n < 3 and m < 3:
                    at = pl.ds(n * POS, POS)
                    block = keep_a[at, pl.ds(mine, WIDTH)] + here_a[at, pl.ds(theirs, WIDTH)]
                elif n < 3:
                    at = pl.ds((2 + n) * POS, POS)
                    block = folded(keep_b, at, g * WIDTH) + folded(here_b, at, (1 - g) * WIDTH)
                else:
                    at = pl.ds((m // 2) * POS, POS)
                    block = folded(keep_b, at, mine) + folded(here_b, at, theirs)
                if n == 0 and m == 0 and g == 0:
                    block = block + unit
                place = lax.rem(x + n, N_COL) * (POS * N_ROW) + group
                out[pl.ds(place, POS, stride=N_ROW), :] = block * scale


def across(a):
    return lax.ppermute(a, "row", [(i, i ^ 1) for i in range(N_ROW)])


def around(a, shift):
    pairs = []
    for r in range(N_ROW):
        for c in range(N_COL):
            to = ((r + 2 * shift) % N_ROW, c) if r % 2 == 0 else (r, (c + shift) % N_COL)
            pairs.append((r * N_COL + c, to[0] * N_COL + to[1]))
    return lax.ppermute(a, ("row", "col"), pairs)


def doubled(a, bit):
    pairs = []
    for r in range(N_ROW):
        for c in range(N_COL):
            to = (r, c ^ bit) if r % 2 == 0 else (r ^ (2 * bit), c)
            pairs.append((r * N_COL + c, to[0] * N_COL + to[1]))
    return lax.ppermute(a, ("row", "col"), pairs)


def after(a, *done):
    return lax.optimization_barrier((a, *done))[0]


def along_z(a, shift):
    pairs = []
    for z in range(N_DOM):
        for r in range(N_ROW):
            to = (z + (shift if r % 2 == 0 else -shift)) % N_DOM
            pairs.append((z * N_ROW + r, to * N_ROW + r))
    return lax.ppermute(a, ("dom", "row"), pairs)


def settled(a, cross):
    pairs = []
    for z in range(N_DOM):
        for r in range(N_ROW):
            to = z if r % 2 == 0 else (z - 1) % N_DOM
            pairs.append((z * N_ROW + r, to * N_ROW + (r ^ cross)))
    return lax.ppermute(a, ("dom", "row"), pairs)


def per_device(protein_panel, tile_mask, domain_class, class_weight):
    tiles, classes = PANEL // TILE, class_weight.shape[0]
    own, sums, weights = call(
        mask_body,
        [(WIDTH, PANEL), (8, PANEL), (1, PANEL)],
        [
            protein_panel.reshape(WIDTH, PANEL),
            tile_mask.reshape(1, tiles),
            domain_class.reshape(1, PANEL),
            class_weight.reshape(1, classes),
        ],
        in_hbm=range(4),
        scratch=[
            pltpu.VMEM((WIDTH, PANEL), F32),
            pltpu.SMEM((1, tiles), jnp.int32),
            pltpu.VMEM((1, PANEL), jnp.int32),
            pltpu.SMEM((1, classes), F32),
            pltpu.SemaphoreType.DMA((4,)),
        ],
    )
    other = across(own)
    chip, again = call(join_body, [(2 * WIDTH, PANEL), (2 * WIDTH + 24, PANEL)], [own, other])
    from_next, from_far, from_last = around(chip, -1), around(chip, 2), around(again, 1)

    def both(a, bit):
        return call(add_body, [(8, PANEL)], [a, doubled(a, bit)])[0]

    sums = across(both(both(sums, 1), 2))
    swap_far = across(after(from_far, sums))
    sums = both(sums, 1)
    swap_next = across(after(from_next, sums))
    early, columns = (3 * WIDTH, PANEL, BF16), (EARLY_COLS, PANEL, BF16)
    a0, a1, ph, pl_, qh, ql = call(
        early_body,
        [(4 * EARLY_ROWS, EARLY_COLS)] * 2 + [early, early, columns, columns],
        [chip, from_next, from_far, swap_next, swap_far, weights],
        mib=16, nbytes=8 << 20,
    )
    came_a = along_z(a0, 1)
    from_last, sums = call(put_body, [(2 * WIDTH + 8, PANEL), (8, PANEL)], [sums, doubled(sums, 2), after(from_last, a0)])
    swap_last = across(from_last)
    b0, b1 = call(
        late_body,
        [(4 * LATE_ROWS + TOTALS, LATE_COLS)] * 2,
        [from_last, swap_last, weights, ph, pl_, qh, ql, sums],
        mib=16, nbytes=0,
        scratch=[pltpu.VMEM((WIDTH + 16, PANEL), BF16)] * 2 + [pltpu.VMEM((PAIR, PANEL), BF16)] * 2,
    )
    came_b = along_z(b0, 1)

    def step(mine, came, rows, totals, shift):
        shape = (rows + totals, mine.shape[1])
        go, stay = call(functools.partial(step_body, half=rows), [shape] * 2, [mine, came])
        return stay, along_z(go, shift)

    a1, came_a = step(a1, came_a, 2 * EARLY_ROWS, 0, 2)
    b1, came_b = step(b1, came_b, 2 * LATE_ROWS, TOTALS, 2)
    a1, came_a = step(a1, came_a, EARLY_ROWS, 0, 4)
    b1, came_b = step(after(b1, a1), came_b, LATE_ROWS, TOTALS, 4)
    give, keep = call(give_early_body, [(3 * POS, EARLY_COLS)] * 2, [a1, came_a])
    ends = [settled(keep, 0), settled(give, 1)]
    give, keep = call(give_late_body, [(5 * POS + TOTALS, LATE_COLS)] * 2, [after(b1, *ends), came_b])
    ends += [settled(keep, 0), settled(give, 1)]
    (flow,) = call(finish_body, [(N_COL * POS * N_ROW, WIDTH)], ends)
    return flow.reshape(1, N_COL, POS, N_ROW, 1, WIDTH)


def solution(mesh):
    placed = (P("row", "col", None, "dom"), P("row", "col", None, "dom"), P("dom"), P())
    return jax.shard_map(
        per_device,
        mesh=mesh,
        in_specs=placed,
        out_specs=P("row", None, "dom", None, "col", None),
        check_vma=False,
    )
```

```python
import functools

import jax
import jax.numpy as jnp
from jax import lax
from jax.experimental import pallas as pl
from jax.experimental.pallas import tpu as pltpu
from jax.sharding import PartitionSpec as P

TILE = 128
N_DOM, N_ROW, N_COL = 16, 8, 4
WIDTH = 128
PANEL = 1024
POS = WIDTH // N_DOM
PAIR = 2 * WIDTH
EARLY_ROWS, EARLY_COLS = 3 * 2 * POS, 3 * PAIR
LATE_ROWS, LATE_COLS = 2 * 2 * POS + 3 * POS, 2 * PAIR
TOTALS = 8
PART = N_COL * POS
ORDER = (7, 3, 5, 1, 6, 2, 4, 0)
PROT = N_ROW * N_COL * WIDTH
VMEM = pl.BlockSpec(memory_space=pltpu.VMEM)
HBM = pl.BlockSpec(memory_space=pltpu.HBM)
F32 = jnp.float32
BF16 = jnp.bfloat16


def call(body, outs, operands, in_hbm=(), mib=4, flops=0, nbytes=1 << 19, scratch=()):
    return pl.pallas_call(
        body,
        out_shape=[
            jax.ShapeDtypeStruct(s[:-1], BF16) if s[-1] is BF16 else jax.ShapeDtypeStruct(s, F32) for s in outs
        ],
        in_specs=[HBM if i in in_hbm else VMEM for i in range(len(operands))],
        out_specs=[VMEM] * len(outs),
        scratch_shapes=list(scratch),
        compiler_params=pltpu.CompilerParams(vmem_limit_bytes=mib << 20),
        cost_estimate=pl.CostEstimate(flops=flops, bytes_accessed=nbytes, transcendentals=0),
    )(*operands)


def core_of():
    return lax.rem(lax.axis_index("row"), 2)


def mask_body(*refs):
    sources, (own, weights), targets, done = refs[:4], refs[4:6], refs[6:10], refs[10]
    copies = [pltpu.make_async_copy(a, b, done.at[i]) for i, (a, b) in enumerate(zip(sources, targets))]
    for copy in copies:
        copy.start()
    for copy in copies[1:]:
        copy.wait()
    panel, tile_mask, classes, class_weight = targets
    of = classes[...]
    found = jnp.zeros((1, PANEL), F32)
    for k in range(class_weight.shape[1]):
        found = jnp.where(of == k, class_weight[0, k], found)
    weights[...] = found
    copies[0].wait()
    for t in range(PANEL // TILE):
        at = pl.ds(t * TILE, TILE)
        kept = panel[:, at] * tile_mask[0, t].astype(F32)
        own[pl.ds(0, WIDTH), at] = kept
        own[pl.ds(WIDTH, 8), at] = jnp.broadcast_to(jnp.sum(kept, axis=0, keepdims=True), (8, TILE))


def join_body(own, other, chip, again, sums):
    for out in (chip, again):
        out[pl.ds(0, WIDTH), :] = own[pl.ds(0, WIDTH), :]
        out[pl.ds(WIDTH, WIDTH), :] = other[pl.ds(0, WIDTH), :]
    sums[...] = own[pl.ds(WIDTH, 8), :] + other[pl.ds(WIDTH, 8), :]


def add_body(a, b, out):
    out[...] = a[...] + b[...]


def split(x):
    high = x.astype(BF16)
    return high, (x - high.astype(F32)).astype(BF16)


def dot3(ah, al, bh, bl):
    dims = (((1,), (1,)), ((), ()))
    dot = functools.partial(lax.dot_general, dimension_numbers=dims, preferred_element_type=F32)
    return dot(ah, bh) + (dot(ah, bl) + dot(al, bh))


def fill_rows(ph, pl_, weights, start, source, swapped):
    z, core = lax.axis_index("dom"), core_of()
    w = weights[...]
    first, second = (WIDTH, 0) if swapped else (0, WIDTH)
    for j, far in enumerate(ORDER):
        at = lax.rem(jnp.where(core == 0, z + far, z + N_DOM - 1 - far), N_DOM) * POS
        mine = source[pl.ds(pl.multiple_of(at + first, POS), POS), :]
        theirs = source[pl.ds(pl.multiple_of(at + second, POS), POS), :]
        to = pl.ds(start + j * 2 * POS, 2 * POS)
        ph[to, :], pl_[to, :] = split(jnp.concatenate([mine, theirs], axis=0) * w)


def fill_columns(qh, ql, start, source, swapped):
    for g in range(2):
        at, of = pl.ds(start + g * WIDTH, WIDTH), pl.ds((1 - g if swapped else g) * WIDTH, WIDTH)
        qh[at, :], ql[at, :] = split(source[of, :])


def early_body(chip, *refs):
    sent, swap, weights = refs[:2], refs[2:4], refs[4]
    outs, (ph, pl_, qh, ql) = refs[5:7], refs[7:]
    core = core_of()
    fill_rows(ph, pl_, weights, 0, chip, False)
    fill_columns(qh, ql, 0, chip, False)

    @pl.when(core == 0)
    def _():
        for i in range(2):
            fill_rows(ph, pl_, weights, (i + 1) * WIDTH, swap[i], True)
            fill_columns(qh, ql, (i + 1) * PAIR, sent[i], False)

    @pl.when(core == 1)
    def _():
        for i in range(2):
            fill_rows(ph, pl_, weights, (i + 1) * WIDTH, sent[i], False)
            fill_columns(qh, ql, (i + 1) * PAIR, swap[i], True)

    block = dot3(ph[...], pl_[...], qh[...], ql[...])
    for i in range(3):
        for j in range(8):
            rows = i * WIDTH + j * 2 * POS
            at = pl.ds((j % 4) * EARLY_ROWS + i * 2 * POS, 2 * POS)
            outs[j // 4][at, :] = block[rows : rows + 2 * POS]


def late_body(sent, swap, weights, ph, pl_, qh, ql, sums, pair, first, second, fh, fl, gh, gl):
    core = core_of()

    @pl.when(core == 0)
    def _():
        fill_rows(fh, fl, weights, 0, swap, True)
        fill_columns(gh, gl, 0, sent, False)

    @pl.when(core == 1)
    def _():
        fill_rows(fh, fl, weights, 0, sent, False)
        fill_columns(gh, gl, 0, swap, True)

    total = (sums[...] + pair[...]) * weights[...]
    at = pl.ds(WIDTH, 16)
    fh[at, :], fl[at, :] = split(jnp.concatenate([total, total], axis=0))
    late_early = dot3(fh[...], fl[...], qh[...], ql[...])
    late_late = dot3(fh[...], fl[...], gh[...], gl[...])
    early_late = dot3(ph[...], pl_[...], gh[...], gl[...])
    for j in range(8):
        out, start = (first, second)[j // 4], (j % 4) * LATE_ROWS
        rows = slice(j * 2 * POS, (j + 1) * 2 * POS)
        out[pl.ds(start, 2 * POS), :] = late_early[rows, : 2 * PAIR]
        at = pl.ds(start + 2 * POS, 2 * POS)
        out[at, pl.ds(0, PAIR)] = late_early[rows, 2 * PAIR :]
        out[at, pl.ds(PAIR, PAIR)] = late_late[rows]
        for i in range(3):
            for g in range(2):
                begin = i * WIDTH + j * 2 * POS + g * POS
                at = pl.ds(start + 4 * POS + i * POS, POS)
                out[at, pl.ds(g * PAIR, PAIR)] = early_late[begin : begin + POS]
    head = late_early[WIDTH : WIDTH + 8, : 2 * PAIR]
    tail = jnp.concatenate([late_early[WIDTH : WIDTH + 8, 2 * PAIR :], late_late[WIDTH : WIDTH + 8]], axis=1)
    odd = lax.broadcasted_iota(jnp.int32, (TOTALS, LATE_COLS), 0) % 2 == 1
    share = jnp.where(odd, tail, head)
    first[pl.ds(4 * LATE_ROWS, TOTALS), :] = share
    second[pl.ds(4 * LATE_ROWS, TOTALS), :] = share


def step_body(mine, came, go, stay, half):
    go[pl.ds(0, half), :] = mine[pl.ds(0, half), :] + came[pl.ds(0, half), :]
    stay[pl.ds(0, half), :] = mine[pl.ds(half, half), :] + came[pl.ds(half, half), :]
    if half < go.shape[0]:
        at = pl.ds(2 * half, TOTALS)
        both = mine[at, :] + came[at, :]
        go[pl.ds(half, TOTALS), :] = both
        stay[pl.ds(half, TOTALS), :] = both


def give_body(mine_a, came_a, mine_b, came_b, give, keep):
    def early(start, to):
        return mine_a[pl.ds(start, POS), to] + came_a[pl.ds(start, POS), to]

    def other(start, to):
        return mine_b[pl.ds(start, POS), to] + came_b[pl.ds(start, POS), to]

    def pairs(k, count=1):
        return pl.ds(k * PAIR, count * PAIR)

    for g, out in enumerate((keep, give)):
        for n in range(3):
            at = pl.ds(n * POS, POS)
            out[at, pairs(0, 3)] = early(n * 2 * POS + g * POS, pairs(0, 3))
            out[at, pairs(3)] = other(4 * POS + n * POS, pairs(g))
        at = pl.ds(3 * POS, POS)
        out[at, pairs(0, 2)] = other(g * POS, pairs(0, 2))
        out[at, pairs(2, 2)] = other(2 * POS + g * POS, pairs(0, 2))
    for k in range(2):
        at = pl.ds(LATE_ROWS + k, 1)
        total = mine_b[at, :] + came_b[at, :]
        for out in (keep, give):
            out[pl.ds(PART, 1), pairs(2 * k, 2)] = total


def finish_body(keep, here, out):
    x, r, z = lax.axis_index("col"), lax.axis_index("row"), lax.axis_index("dom")
    core = lax.rem(r, 2)
    y = lax.div(r, 2)
    lanes = lax.broadcasted_iota(jnp.int32, (POS, WIDTH), 1)
    rows = lax.broadcasted_iota(jnp.int32, (POS, WIDTH), 0)
    unit = (lanes == z * POS + rows).astype(F32)
    for m in range(4):
        for g in range(2):
            mine, theirs = pl.ds(m * PAIR + g * WIDTH, WIDTH), pl.ds(m * PAIR + (1 - g) * WIDTH, WIDTH)
            total = keep[pl.ds(PART, 1), mine] + here[pl.ds(PART, 1), theirs]
            scale = PROT / (total + 1.0)
            group = 2 * lax.rem(y + m, 4) + (core if g == 0 else 1 - core)
            for n in range(N_COL):
                at = pl.ds(n * POS, POS)
                block = keep[at, mine] + here[at, theirs]
                if n == 0 and m == 0 and g == 0:
                    block = block + unit
                place = lax.rem(x + n, N_COL) * (POS * N_ROW) + group
                out[pl.ds(place, POS, stride=N_ROW), :] = block * scale


def across(a):
    return lax.ppermute(a, "row", [(i, i ^ 1) for i in range(N_ROW)])


def around(a, shift):
    pairs = []
    for r in range(N_ROW):
        for c in range(N_COL):
            to = ((r + 2 * shift) % N_ROW, c) if r % 2 == 0 else (r, (c + shift) % N_COL)
            pairs.append((r * N_COL + c, to[0] * N_COL + to[1]))
    return lax.ppermute(a, ("row", "col"), pairs)


def doubled(a, bit):
    pairs = []
    for r in range(N_ROW):
        for c in range(N_COL):
            to = (r, c ^ bit) if r % 2 == 0 else (r ^ (2 * bit), c)
            pairs.append((r * N_COL + c, to[0] * N_COL + to[1]))
    return lax.ppermute(a, ("row", "col"), pairs)


def after(a, *done):
    return lax.optimization_barrier((a, *done))[0]


def along_z(a, shift):
    pairs = []
    for z in range(N_DOM):
        for r in range(N_ROW):
            to = (z + (shift if r % 2 == 0 else -shift)) % N_DOM
            pairs.append((z * N_ROW + r, to * N_ROW + r))
    return lax.ppermute(a, ("dom", "row"), pairs)


def settled(a, cross):
    pairs = []
    for z in range(N_DOM):
        for r in range(N_ROW):
            to = z if r % 2 == 0 else (z - 1) % N_DOM
            pairs.append((z * N_ROW + r, to * N_ROW + (r ^ cross)))
    return lax.ppermute(a, ("dom", "row"), pairs)


def per_device(protein_panel, tile_mask, domain_class, class_weight):
    tiles, classes = PANEL // TILE, class_weight.shape[0]
    own, weights = call(
        mask_body,
        [(WIDTH + 8, PANEL), (1, PANEL)],
        [
            protein_panel.reshape(WIDTH, PANEL),
            tile_mask.reshape(1, tiles),
            domain_class.reshape(1, PANEL),
            class_weight.reshape(1, classes),
        ],
        in_hbm=range(4),
        scratch=[
            pltpu.VMEM((WIDTH, PANEL), F32),
            pltpu.SMEM((1, tiles), jnp.int32),
            pltpu.VMEM((1, PANEL), jnp.int32),
            pltpu.SMEM((1, classes), F32),
            pltpu.SemaphoreType.DMA((4,)),
        ],
    )
    other = across(own)
    chip, again, sums = call(
        join_body,
        [(2 * WIDTH, PANEL), (2 * WIDTH + 24, PANEL), (8, PANEL)],
        [own, other],
    )
    from_next, from_far, from_last = around(chip, -1), around(chip, 2), around(again, 1)

    def both(a, bit):
        return call(add_body, [(8, PANEL)], [a, doubled(a, bit)])[0]

    sums = across(both(both(sums, 1), 2))
    swap_far = across(after(from_far, sums))
    sums = both(sums, 1)
    swap_next = across(after(from_next, sums))

    early, columns = (3 * WIDTH, PANEL, BF16), (EARLY_COLS, PANEL, BF16)
    a0, a1, ph, pl_, qh, ql = call(
        early_body,
        [(4 * EARLY_ROWS, EARLY_COLS)] * 2 + [early, early, columns, columns],
        [chip, from_next, from_far, swap_next, swap_far, weights],
        mib=16, nbytes=8 << 20,
    )
    came_a = along_z(a0, 1)
    pair = doubled(sums, 2)
    swap_last = across(after(from_last, a0, pair))
    b0, b1 = call(
        late_body,
        [(4 * LATE_ROWS + TOTALS, LATE_COLS)] * 2,
        [from_last, swap_last, weights, ph, pl_, qh, ql, sums, pair],
        mib=16, nbytes=0,
        scratch=[pltpu.VMEM((WIDTH + 16, PANEL), BF16)] * 2 + [pltpu.VMEM((PAIR, PANEL), BF16)] * 2,
    )
    came_b = along_z(b0, 1)

    def step(mine, came, rows, totals, shift):
        shape = (rows + totals, mine.shape[1])
        go, stay = call(functools.partial(step_body, half=rows), [shape] * 2, [mine, came])
        return stay, along_z(go, shift)

    a1, came_a = step(a1, came_a, 2 * EARLY_ROWS, 0, 2)
    b1, came_b = step(b1, came_b, 2 * LATE_ROWS, TOTALS, 2)
    a1, came_a = step(a1, came_a, EARLY_ROWS, 0, 4)
    b1, came_b = step(b1, came_b, LATE_ROWS, TOTALS, 4)
    give, keep = call(give_body, [(PART + TOTALS, 4 * PAIR)] * 2, [a1, came_a, b1, came_b])
    (flow,) = call(finish_body, [(N_COL * POS * N_ROW, WIDTH)], [settled(keep, 0), settled(give, 1)])
    return flow.reshape(1, N_COL, POS, N_ROW, 1, WIDTH)


def solution(mesh):
    placed = (P("row", "col", None, "dom"), P("row", "col", None, "dom"), P("dom"), P())
    return jax.shard_map(
        per_device,
        mesh=mesh,
        in_specs=placed,
        out_specs=P("row", None, "dom", None, "col", None),
        check_vma=False,
    )
```

```python
import functools

import jax
import jax.numpy as jnp
from jax import lax
from jax.experimental import pallas as pl
from jax.experimental.pallas import tpu as pltpu
from jax.sharding import PartitionSpec as P

TILE = 128
N_DOM, N_ROW, N_COL = 16, 8, 4
WIDTH = 128
PANEL = 1024
POS = WIDTH // N_DOM
PAIR = 2 * WIDTH
EARLY_ROWS, EARLY_COLS = 3 * 2 * POS, 3 * PAIR
LATE_ROWS, LATE_COLS = 2 * 2 * POS + 3 * POS, 2 * PAIR
TOTALS = 8
PART = N_COL * POS
ORDER = (7, 3, 5, 1, 6, 2, 4, 0)
PROT = N_ROW * N_COL * WIDTH
VMEM = pl.BlockSpec(memory_space=pltpu.VMEM)
HBM = pl.BlockSpec(memory_space=pltpu.HBM)
F32 = jnp.float32
BF16 = jnp.bfloat16


def call(body, outs, operands, in_hbm=(), mib=4, flops=0, nbytes=1 << 19, scratch=()):
    return pl.pallas_call(
        body,
        out_shape=[
            jax.ShapeDtypeStruct(s[:-1], BF16) if s[-1] is BF16 else jax.ShapeDtypeStruct(s, F32) for s in outs
        ],
        in_specs=[HBM if i in in_hbm else VMEM for i in range(len(operands))],
        out_specs=[VMEM] * len(outs),
        scratch_shapes=list(scratch),
        compiler_params=pltpu.CompilerParams(vmem_limit_bytes=mib << 20),
        cost_estimate=pl.CostEstimate(flops=flops, bytes_accessed=nbytes, transcendentals=0),
    )(*operands)


def core_of():
    return lax.rem(lax.axis_index("row"), 2)


def mask_body(*refs):
    sources, (own, weights), targets, done = refs[:4], refs[4:6], refs[6:10], refs[10]
    copies = [pltpu.make_async_copy(a, b, done.at[i]) for i, (a, b) in enumerate(zip(sources, targets))]
    for copy in copies:
        copy.start()
    for copy in copies[1:]:
        copy.wait()
    panel, tile_mask, classes, class_weight = targets
    of = classes[...]
    found = jnp.zeros((1, PANEL), F32)
    for k in range(class_weight.shape[1]):
        found = jnp.where(of == k, class_weight[0, k], found)
    weights[...] = found
    copies[0].wait()
    for t in range(PANEL // TILE):
        at = pl.ds(t * TILE, TILE)
        kept = panel[:, at] * tile_mask[0, t].astype(F32)
        own[pl.ds(0, WIDTH), at] = kept
        own[pl.ds(WIDTH, 8), at] = jnp.broadcast_to(jnp.sum(kept, axis=0, keepdims=True), (8, TILE))


def join_body(own, other, chip, again, sums):
    for out in (chip, again):
        out[pl.ds(0, WIDTH), :] = own[pl.ds(0, WIDTH), :]
        out[pl.ds(WIDTH, WIDTH), :] = other[pl.ds(0, WIDTH), :]
    sums[...] = own[pl.ds(WIDTH, 8), :] + other[pl.ds(WIDTH, 8), :]


def add_body(a, b, out):
    out[...] = a[...] + b[...]


def split(x):
    high = x.astype(BF16)
    return high, (x - high.astype(F32)).astype(BF16)


def dot3(ah, al, bh, bl):
    dims = (((1,), (1,)), ((), ()))
    dot = functools.partial(lax.dot_general, dimension_numbers=dims, preferred_element_type=F32)
    return dot(ah, bh) + (dot(ah, bl) + dot(al, bh))


def fill_rows(ph, pl_, weights, start, source, swapped):
    z, core = lax.axis_index("dom"), core_of()
    w = weights[...]
    first, second = (WIDTH, 0) if swapped else (0, WIDTH)
    for j, far in enumerate(ORDER):
        at = lax.rem(jnp.where(core == 0, z + far, z + N_DOM - 1 - far), N_DOM) * POS
        mine = source[pl.ds(pl.multiple_of(at + first, POS), POS), :]
        theirs = source[pl.ds(pl.multiple_of(at + second, POS), POS), :]
        to = pl.ds(start + j * 2 * POS, 2 * POS)
        ph[to, :], pl_[to, :] = split(jnp.concatenate([mine, theirs], axis=0) * w)


def fill_columns(qh, ql, start, source, swapped):
    for g in range(2):
        at, of = pl.ds(start + g * WIDTH, WIDTH), pl.ds((1 - g if swapped else g) * WIDTH, WIDTH)
        qh[at, :], ql[at, :] = split(source[of, :])


def early_body(chip, *refs):
    sent, swap, weights = refs[:2], refs[2:4], refs[4]
    outs, (ph, pl_, qh, ql) = refs[5:7], refs[7:]
    core = core_of()
    fill_rows(ph, pl_, weights, 0, chip, False)
    fill_columns(qh, ql, 0, chip, False)

    @pl.when(core == 0)
    def _():
        for i in range(2):
            fill_rows(ph, pl_, weights, (i + 1) * WIDTH, swap[i], True)
            fill_columns(qh, ql, (i + 1) * PAIR, sent[i], False)

    @pl.when(core == 1)
    def _():
        for i in range(2):
            fill_rows(ph, pl_, weights, (i + 1) * WIDTH, sent[i], False)
            fill_columns(qh, ql, (i + 1) * PAIR, swap[i], True)

    block = dot3(ph[...], pl_[...], qh[...], ql[...])
    for i in range(3):
        for j in range(8):
            rows = i * WIDTH + j * 2 * POS
            at = pl.ds((j % 4) * EARLY_ROWS + i * 2 * POS, 2 * POS)
            outs[j // 4][at, :] = block[rows : rows + 2 * POS]


def late_body(sent, swap, weights, ph, pl_, qh, ql, sums, pair, first, second, fh, fl, gh, gl):
    core = core_of()

    @pl.when(core == 0)
    def _():
        fill_rows(fh, fl, weights, 0, swap, True)
        fill_columns(gh, gl, 0, sent, False)

    @pl.when(core == 1)
    def _():
        fill_rows(fh, fl, weights, 0, sent, False)
        fill_columns(gh, gl, 0, swap, True)

    total = (sums[...] + pair[...]) * weights[...]
    at = pl.ds(WIDTH, 16)
    fh[at, :], fl[at, :] = split(jnp.concatenate([total, total], axis=0))
    late_early = dot3(fh[...], fl[...], qh[...], ql[...])
    late_late = dot3(fh[...], fl[...], gh[...], gl[...])
    early_late = dot3(ph[...], pl_[...], gh[...], gl[...])
    for j in range(8):
        out, start = (first, second)[j // 4], (j % 4) * LATE_ROWS
        rows = slice(j * 2 * POS, (j + 1) * 2 * POS)
        out[pl.ds(start, 2 * POS), :] = late_early[rows, : 2 * PAIR]
        at = pl.ds(start + 2 * POS, 2 * POS)
        out[at, pl.ds(0, PAIR)] = late_early[rows, 2 * PAIR :]
        out[at, pl.ds(PAIR, PAIR)] = late_late[rows]
        for i in range(3):
            for g in range(2):
                begin = i * WIDTH + j * 2 * POS + g * POS
                at = pl.ds(start + 4 * POS + i * POS, POS)
                out[at, pl.ds(g * PAIR, PAIR)] = early_late[begin : begin + POS]
    head = late_early[WIDTH : WIDTH + 8, : 2 * PAIR]
    tail = jnp.concatenate([late_early[WIDTH : WIDTH + 8, 2 * PAIR :], late_late[WIDTH : WIDTH + 8]], axis=1)
    odd = lax.broadcasted_iota(jnp.int32, (TOTALS, LATE_COLS), 0) % 2 == 1
    share = jnp.where(odd, tail, head)
    first[pl.ds(4 * LATE_ROWS, TOTALS), :] = share
    second[pl.ds(4 * LATE_ROWS, TOTALS), :] = share


def step_body(mine, came, go, stay, half):
    go[pl.ds(0, half), :] = mine[pl.ds(0, half), :] + came[pl.ds(0, half), :]
    stay[pl.ds(0, half), :] = mine[pl.ds(half, half), :] + came[pl.ds(half, half), :]
    if half < go.shape[0]:
        at = pl.ds(2 * half, TOTALS)
        both = mine[at, :] + came[at, :]
        go[pl.ds(half, TOTALS), :] = both
        stay[pl.ds(half, TOTALS), :] = both


def give_body(mine_a, came_a, mine_b, came_b, give, keep):
    def early(start, to):
        return mine_a[pl.ds(start, POS), to] + came_a[pl.ds(start, POS), to]

    def other(start, to):
        return mine_b[pl.ds(start, POS), to] + came_b[pl.ds(start, POS), to]

    def pairs(k, count=1):
        return pl.ds(k * PAIR, count * PAIR)

    for g, out in enumerate((keep, give)):
        for n in range(3):
            at = pl.ds(n * POS, POS)
            out[at, pairs(0, 3)] = early(n * 2 * POS + g * POS, pairs(0, 3))
            out[at, pairs(3)] = other(4 * POS + n * POS, pairs(g))
        at = pl.ds(3 * POS, POS)
        out[at, pairs(0, 2)] = other(g * POS, pairs(0, 2))
        out[at, pairs(2, 2)] = other(2 * POS + g * POS, pairs(0, 2))
    for k in range(2):
        at = pl.ds(LATE_ROWS + k, 1)
        total = mine_b[at, :] + came_b[at, :]
        for out in (keep, give):
            out[pl.ds(PART, 1), pairs(2 * k, 2)] = total


def finish_body(keep, here, out):
    x, r, z = lax.axis_index("col"), lax.axis_index("row"), lax.axis_index("dom")
    core = lax.rem(r, 2)
    y = lax.div(r, 2)
    lanes = lax.broadcasted_iota(jnp.int32, (POS, WIDTH), 1)
    rows = lax.broadcasted_iota(jnp.int32, (POS, WIDTH), 0)
    unit = (lanes == z * POS + rows).astype(F32)
    for m in range(4):
        for g in range(2):
            mine, theirs = pl.ds(m * PAIR + g * WIDTH, WIDTH), pl.ds(m * PAIR + (1 - g) * WIDTH, WIDTH)
            total = keep[pl.ds(PART, 1), mine] + here[pl.ds(PART, 1), theirs]
            scale = PROT / (total + 1.0)
            group = 2 * lax.rem(y + m, 4) + (core if g == 0 else 1 - core)
            for n in range(N_COL):
                at = pl.ds(n * POS, POS)
                block = keep[at, mine] + here[at, theirs]
                if n == 0 and m == 0 and g == 0:
                    block = block + unit
                place = lax.rem(x + n, N_COL) * (POS * N_ROW) + group
                out[pl.ds(place, POS, stride=N_ROW), :] = block * scale


def across(a):
    return lax.ppermute(a, "row", [(i, i ^ 1) for i in range(N_ROW)])


def around(a, shift):
    pairs = []
    for r in range(N_ROW):
        for c in range(N_COL):
            to = ((r + 2 * shift) % N_ROW, c) if r % 2 == 0 else (r, (c + shift) % N_COL)
            pairs.append((r * N_COL + c, to[0] * N_COL + to[1]))
    return lax.ppermute(a, ("row", "col"), pairs)


def doubled(a, bit):
    pairs = []
    for r in range(N_ROW):
        for c in range(N_COL):
            to = (r, c ^ bit) if r % 2 == 0 else (r ^ (2 * bit), c)
            pairs.append((r * N_COL + c, to[0] * N_COL + to[1]))
    return lax.ppermute(a, ("row", "col"), pairs)


def after(a, *done):
    return lax.optimization_barrier((a, *done))[0]


def along_z(a, shift):
    pairs = []
    for z in range(N_DOM):
        for r in range(N_ROW):
            to = (z + (shift if r % 2 == 0 else -shift)) % N_DOM
            pairs.append((z * N_ROW + r, to * N_ROW + r))
    return lax.ppermute(a, ("dom", "row"), pairs)


def settled(a, cross):
    pairs = []
    for z in range(N_DOM):
        for r in range(N_ROW):
            to = z if r % 2 == 0 else (z - 1) % N_DOM
            pairs.append((z * N_ROW + r, to * N_ROW + (r ^ cross)))
    return lax.ppermute(a, ("dom", "row"), pairs)


def per_device(protein_panel, tile_mask, domain_class, class_weight):
    tiles, classes = PANEL // TILE, class_weight.shape[0]
    own, weights = call(
        mask_body,
        [(WIDTH + 8, PANEL), (1, PANEL)],
        [
            protein_panel.reshape(WIDTH, PANEL),
            tile_mask.reshape(1, tiles),
            domain_class.reshape(1, PANEL),
            class_weight.reshape(1, classes),
        ],
        in_hbm=range(4), mib=62,
        scratch=[
            pltpu.VMEM((WIDTH, PANEL), F32),
            pltpu.SMEM((1, tiles), jnp.int32),
            pltpu.VMEM((1, PANEL), jnp.int32),
            pltpu.SMEM((1, classes), F32),
            pltpu.SemaphoreType.DMA((4,)),
        ],
    )
    other = across(own)
    chip, again, sums = call(
        join_body,
        [(2 * WIDTH, PANEL), (2 * WIDTH + 24, PANEL), (8, PANEL)],
        [own, other],
    )
    from_next, from_far, from_last = around(chip, -1), around(chip, 2), around(again, 1)

    def both(a, bit):
        return call(add_body, [(8, PANEL)], [a, doubled(a, bit)])[0]

    sums = across(both(both(sums, 1), 2))
    swap_far = across(after(from_far, sums))
    sums = both(sums, 1)
    swap_next = across(after(from_next, sums))

    early, columns = (3 * WIDTH, PANEL, BF16), (EARLY_COLS, PANEL, BF16)
    a0, a1, ph, pl_, qh, ql = call(
        early_body,
        [(4 * EARLY_ROWS, EARLY_COLS)] * 2 + [early, early, columns, columns],
        [chip, from_next, from_far, swap_next, swap_far, weights],
        mib=16, nbytes=8 << 20,
    )
    came_a = along_z(a0, 1)
    pair = doubled(sums, 2)
    swap_last = across(after(from_last, a0, pair))
    b0, b1 = call(
        late_body,
        [(4 * LATE_ROWS + TOTALS, LATE_COLS)] * 2,
        [from_last, swap_last, weights, ph, pl_, qh, ql, sums, pair],
        mib=16, nbytes=0,
        scratch=[pltpu.VMEM((WIDTH + 16, PANEL), BF16)] * 2 + [pltpu.VMEM((PAIR, PANEL), BF16)] * 2,
    )
    came_b = along_z(b0, 1)

    def step(mine, came, rows, totals, shift):
        shape = (rows + totals, mine.shape[1])
        go, stay = call(functools.partial(step_body, half=rows), [shape] * 2, [mine, came])
        return stay, along_z(go, shift)

    a1, came_a = step(a1, came_a, 2 * EARLY_ROWS, 0, 2)
    b1, came_b = step(b1, came_b, 2 * LATE_ROWS, TOTALS, 2)
    a1, came_a = step(a1, came_a, EARLY_ROWS, 0, 4)
    b1, came_b = step(b1, came_b, LATE_ROWS, TOTALS, 4)
    give, keep = call(give_body, [(PART + TOTALS, 4 * PAIR)] * 2, [a1, came_a, b1, came_b])
    (flow,) = call(finish_body, [(N_COL * POS * N_ROW, WIDTH)], [settled(keep, 0), settled(give, 1)])
    return flow.reshape(1, N_COL, POS, N_ROW, 1, WIDTH)


def solution(mesh):
    placed = (P("row", "col", None, "dom"), P("row", "col", None, "dom"), P("dom"), P())
    return jax.shard_map(
        per_device,
        mesh=mesh,
        in_specs=placed,
        out_specs=P("row", None, "dom", None, "col", None),
        check_vma=False,
    )
```
